128 devices in a mesh: rows: 32 (over y, z, core), sub: 4 (over x).
Axes of the slice: x: 4, y: 4, z: 4, core: 2. Of those that a mesh axis runs over, the one named last changes fastest.
Arguments:
- windows: bfloat16 [2097152, 512], P(('rows', 'sub')), may hold values from -7 to 7
- landmark_index: int32 [512], replicated, may hold values from 0 to 2097151, as said below
- start_basis: float32 [512, 64], replicated, may hold values from -6 to 6
Outputs:
- embedding: float32 [64, 2097152], P(None, ('rows', 'sub'))
- basis: float32 [512, 64], replicated
The draws below stay inside these ranges and needn't reach their ends.
Inputs may be any that keep to these rules, and one draw needn't show every extreme that they name: `landmark_index`: both the first and the last window are named in every draw.
All inputs are finite; a program needn't handle non-finite values.
Results may differ from the reference program's by a relative error of at most 0.0021.
Values sent between devices are 32-bit elements; how exact they have to be, the bound alone decides.
No kernel may reach another device: no remote copies, remote signals or barrier semaphores. Data moves between devices by JAX's collectives and lax.ppermute only.
A program may use at most 128 MiB of HBM per device.

```python
import math
import jax
import jax.numpy as jnp
from jax import lax

E = 512
M = 512
K = 64
ITERS = 8
WINDOWS = 2097152


def draw_windows(key, part):
    key = jax.random.fold_in(key, 11)
    keys = jax.random.split(key, 4)
    clusters = M // 4
    centers = jnp.clip(jax.random.normal(keys[0], (clusters, E), jnp.float32), -3.0, 3.0)
    spread = jnp.exp(jax.random.uniform(keys[1], (clusters,), jnp.float32, math.log(0.5), math.log(1.2)))
    member = jax.random.randint(keys[2], (WINDOWS,), 0, clusters, dtype=jnp.int32)
    noise = jnp.clip(jax.random.normal(keys[3], (WINDOWS, E), jnp.float32), -3.0, 3.0)
    values = centers[member] + spread[member][:, None] * noise
    return values.astype(jnp.bfloat16)


def draw_landmark_index(key, part):
    key = jax.random.fold_in(key, 7)
    limit = WINDOWS
    picks = jax.random.randint(key, (M,), 0, limit, dtype=jnp.int32)
    picks = picks.at[0].set(limit - 1)
    picks = picks.at[1].set(0)
    return picks


def scatter_about(rng, dims, scale, most, kind=jnp.bfloat16):
    entries = scale * jax.random.normal(rng, dims, jnp.float32)
    return jnp.clip(entries, min=-most, max=most).astype(kind)


def setup_inputs(seed: int = 0) -> dict:
    seeds = jax.random.split(jax.random.key(seed), 4)
    windows = draw_windows(jax.random.fold_in(seeds[3], 71), 0)
    landmark_index = draw_landmark_index(jax.random.fold_in(seeds[3], 71), 0)
    start_basis = scatter_about(seeds[2], (M, K), 1.0, 6.0, jnp.float32)
    return dict(windows=windows, landmark_index=landmark_index, start_basis=start_basis)


sharpness = 6.0
epsilon = 1e-06

def inverse_norm(values):
    data = values.astype(jnp.float32)
    return lax.rsqrt(lax.optimization_barrier(jnp.mean(data * data, axis=1)) + epsilon)

def scaled_block(block, landmarks, land_inverse):
    products = jnp.dot(block.astype(jnp.float32), landmarks.T.astype(jnp.float32), preferred_element_type=jnp.float32)
    cosine = products * inverse_norm(block)[:, None] * land_inverse[None, :] / E
    affinity = jnp.exp(sharpness * cosine)
    row_degree = lax.optimization_barrier(jnp.sum(affinity, axis=1))
    scaled = (affinity * lax.rsqrt(row_degree)[:, None]).astype(jnp.bfloat16)
    return (affinity, scaled)

def reference(windows, landmark_index, start_basis):
    landmarks = jnp.take(windows, landmark_index.astype(jnp.int32), axis=0)
    land_inverse = inverse_norm(landmarks)
    count = windows.shape[0]
    block_rows = min(count, 8192)
    blocks = windows.reshape(count // block_rows, block_rows, E)

    def accumulate(carry, block):
        affinity, scaled = scaled_block(block, landmarks, land_inverse)
        cross = carry[0] + jnp.dot(scaled.T.astype(jnp.float32), scaled.astype(jnp.float32), preferred_element_type=jnp.float32)
        column = carry[1] + lax.optimization_barrier(jnp.sum(affinity, axis=0))
        return ((cross, column), None)
    start = (jnp.zeros((M, M), jnp.float32), jnp.zeros((M,), jnp.float32))
    (cross, column_degree), _ = lax.scan(accumulate, start, blocks)
    column_inverse = lax.rsqrt(column_degree)
    gram = cross * column_inverse[:, None] * column_inverse[None, :]
    basis = start_basis
    for step in range(ITERS):
        image = jnp.dot(gram, basis, precision=lax.Precision.HIGHEST)
        square = jnp.dot(image.T, image, precision=lax.Precision.HIGHEST)
        lower = jnp.linalg.cholesky(square)
        basis = jax.scipy.linalg.solve_triangular(lower, image.T, lower=True).T
    weighted = (basis * column_inverse[:, None]).astype(jnp.bfloat16)

    def project(block):
        affinity, scaled = scaled_block(block, landmarks, land_inverse)
        return lax.dot_general(weighted.astype(jnp.float32), scaled.astype(jnp.float32), (((0,), (1,)), ((), ())), preferred_element_type=jnp.float32)
    pieces = lax.map(project, blocks)
    embedding = jnp.transpose(pieces, (1, 0, 2)).reshape(K, count)
    return (embedding, basis)
```

```python
import functools

import jax
import jax.numpy as jnp
import numpy as np
from jax import lax
from jax.experimental import pallas as pl
from jax.experimental.pallas import tpu as pltpu
from jax.sharding import PartitionSpec as P

ITERS = 8
BLOCK = 2048
SUB = 512
LANES = 128
CHUNK = 16

sharpness = 6.0
epsilon = 1e-06
LOG2E = 1.4426950408889634
HIGHEST = lax.Precision.HIGHEST


def dot(a, b, dims, precision=None):
    return lax.dot_general(
        a, b, (dims, ((), ())), precision=precision, preferred_element_type=jnp.float32
    )


NN = ((1,), (0,))
NT = ((1,), (1,))


def pick_kernel(shifted, windows, out, held, sem):
    count = shifted.shape[0]
    rows_here, width = windows.shape
    parts = width // LANES
    out[...] = jnp.zeros_like(out)

    def block_copy(j):
        start = pl.multiple_of((shifted[j] // 16) * 16, 16)
        return pltpu.make_async_copy(
            windows.at[pl.ds(start, 16), :], held.at[j], sem
        )

    def inside(j):
        return (shifted[j] >= 0) & (shifted[j] < rows_here)

    def begin(j, carry):
        @pl.when(inside(j))
        def _():
            block_copy(j).start()

        return carry

    def finish(j, carry):
        @pl.when(inside(j))
        def _():
            block_copy(j).wait()

        return carry

    def place(j, carry):
        @pl.when(inside(j))
        def _():
            block = held[j].astype(jnp.float32)
            row = lax.broadcasted_iota(jnp.int32, block.shape, 0)
            row = jnp.sum(jnp.where(row == shifted[j] % 16, block, 0.0), axis=0, keepdims=True)
            for c in range(parts):
                out[pl.ds(parts * j + c, 1), :] = row[:, c * LANES : (c + 1) * LANES]

        return carry

    lax.fori_loop(0, count, begin, 0, unroll=8)
    lax.fori_loop(0, count, finish, 0, unroll=8)
    lax.fori_loop(0, count, place, 0)


def pick(shifted, windows):
    count, width = shifted.shape[0], windows.shape[1]
    return pl.pallas_call(
        pick_kernel,
        out_shape=jax.ShapeDtypeStruct((count * width // LANES, LANES), jnp.float32),
        in_specs=[
            pl.BlockSpec(memory_space=pltpu.SMEM),
            pl.BlockSpec(memory_space=pl.ANY),
        ],
        out_specs=pl.BlockSpec(memory_space=pltpu.VMEM),
        scratch_shapes=[
            pltpu.VMEM((count, 16, width), jnp.bfloat16),
            pltpu.SemaphoreType.DMA,
        ],
        compiler_params=pltpu.CompilerParams(vmem_limit_bytes=32 * 2**20),
    )(shifted, windows)


def main_kernel(marks, windows, scaled, packed, land, land_scale, cross, column):
    step = pl.program_id(0)
    count, width = land.shape
    half = count // 2
    parts = width // LANES

    @pl.when(step == 0)
    def _():
        square = jnp.zeros((count, 1), jnp.float32)
        for c in range(parts):
            piece = marks[pl.ds(c, count, stride=parts), :]
            land[:, c * LANES : (c + 1) * LANES] = piece.astype(jnp.bfloat16)
            square += jnp.sum(piece * piece, axis=1, keepdims=True)
        inverse = lax.rsqrt(square / width + epsilon)
        land_scale[...] = jnp.broadcast_to(
            inverse * (sharpness * LOG2E / width), land_scale.shape
        )
        cross[...] = jnp.zeros_like(cross)
        column[...] = jnp.zeros_like(column)

    for t in range(BLOCK // SUB):
        part = slice(t * SUB, (t + 1) * SUB)
        data = windows[part, :]
        products = dot(land[...], data, NT)
        wide = data.astype(jnp.float32)
        mean = jnp.sum(wide * wide, axis=1, keepdims=True) / width
        inverse = jnp.transpose(jnp.broadcast_to(lax.rsqrt(mean + epsilon), (SUB, LANES)))[:1]
        scale = jnp.concatenate([land_scale[...]] * (SUB // LANES), axis=1)
        affinity = jnp.exp2(products * scale * inverse)
        total = jnp.sum(affinity, axis=0, keepdims=True)
        lanes = affinity[:, :LANES]
        for c in range(1, SUB // LANES):
            lanes += affinity[:, c * LANES : (c + 1) * LANES]
        column[...] += lanes
        rounded = (affinity * lax.rsqrt(total)).astype(jnp.bfloat16)
        scaled[:, part] = rounded
        low, high = rounded[:half], rounded[half:]
        cross[0] += dot(low, low, NT)
        cross[1] += dot(high, low, NT)
        cross[2] += dot(high, high, NT)

    @pl.when(step == pl.num_programs(0) - 1)
    def _():
        packed[...] = jnp.zeros_like(packed)
        at = 0
        for b in range(3):
            for c in range(half // LANES):
                packed[at : at + half, :] = cross[b, :, c * LANES : (c + 1) * LANES]
                at += half
        for c in range(count // LANES):
            turned = jnp.transpose(column[c * LANES : (c + 1) * LANES, :])
            packed[at : at + 1, :] = jnp.sum(turned, axis=0, keepdims=True)
            at += 1


def main_pass(marks, windows, total_rows):
    rows_here, width = windows.shape
    count = marks.shape[0] * LANES // width
    half = count // 2
    return pl.pallas_call(
        main_kernel,
        grid=(rows_here // BLOCK,),
        out_shape=(
            jax.ShapeDtypeStruct((count, rows_here), jnp.bfloat16),
            jax.ShapeDtypeStruct((total_rows, LANES), jnp.float32),
        ),
        in_specs=[
            pl.BlockSpec(marks.shape, lambda i: (0, 0)),
            pl.BlockSpec((BLOCK, width), lambda i: (i, 0)),
        ],
        out_specs=(
            pl.BlockSpec((count, BLOCK), lambda i: (0, i)),
            pl.BlockSpec((total_rows, LANES), lambda i: (0, 0)),
        ),
        scratch_shapes=[
            pltpu.VMEM((count, width), jnp.bfloat16),
            pltpu.VMEM((count, LANES), jnp.float32),
            pltpu.VMEM((3, half, half), jnp.float32),
            pltpu.VMEM((count, LANES), jnp.float32),
        ],
        compiler_params=pltpu.CompilerParams(
            dimension_semantics=("arbitrary",), vmem_limit_bytes=48 * 2**20
        ),
    )(marks, windows)


def inverse_cholesky(square):
    size = square.shape[0]
    row = lax.broadcasted_iota(jnp.int32, (size, 2 * size), 0)
    lane = lax.broadcasted_iota(jnp.int32, (size, 2 * size), 1)
    table = jnp.concatenate([square, jnp.zeros_like(square)], axis=1)
    table = jnp.where(lane == row + size, 1.0, table)
    pivots = jnp.zeros((size, 1), jnp.float32)
    for k in range(size):
        pivot_row = table[k : k + 1, :]
        column = table[:, k : k + 1]
        pivot = table[k : k + 1, k : k + 1]
        factor = jnp.where(row[:, :1] > k, column / pivot, 0.0)
        pivots = jnp.where(row[:, :1] == k, pivot, pivots)
        table = table - factor * pivot_row
    return table[:, size:] * lax.rsqrt(pivots)


def embed_kernel(packed, start, scaled, embedding, basis, gram, held, staged, in_sem, out_sem):
    count = gram.shape[0]
    half = count // 2
    blocks = held.shape[0]
    block = held.shape[2]
    reads = [
        pltpu.make_async_copy(
            scaled.at[:, pl.ds(b * block, block)], held.at[b], in_sem.at[b]
        )
        for b in range(blocks)
    ]
    for read in reads:
        read.start()

    base = 3 * half * (half // LANES)
    degree = jnp.concatenate(
        [packed[base + c : base + c + 1, :] for c in range(count // LANES)], axis=1
    )
    across = lax.rsqrt(degree)
    down = jnp.concatenate(
        [
            jnp.transpose(
                jnp.broadcast_to(across[:, c * LANES : (c + 1) * LANES], (LANES, LANES))
            )
            for c in range(count // LANES)
        ],
        axis=0,
    )

    def corner(b):
        at = b * half * (half // LANES)
        return jnp.concatenate(
            [packed[at + c * half : at + (c + 1) * half, :] for c in range(half // LANES)],
            axis=1,
        )

    wide = jnp.concatenate([down[:, :1]] * 1, axis=1)
    low = corner(0) * wide[:half] * across[:, :half]
    side = corner(1) * wide[half:] * across[:, :half]
    high = corner(2) * wide[half:] * across[:, half:]
    gram[:half, :half] = low
    gram[half:, :half] = side
    gram[:half, half:] = jnp.transpose(side)
    gram[half:, half:] = high

    def iterate(_, turned):
        image = dot(turned, gram[...], NN, HIGHEST)
        square = dot(image, image, NT, HIGHEST)
        return dot(inverse_cholesky(square), image, NN, HIGHEST)

    turned = lax.fori_loop(0, ITERS, iterate, jnp.transpose(start[...]))
    basis[...] = jnp.transpose(turned)
    weighted = (turned * across).astype(jnp.bfloat16)
    writes = []
    for b in range(blocks):
        reads[b].wait()
        staged[:, b * block : (b + 1) * block] = dot(weighted, held[b], NN)
        write = pltpu.make_async_copy(
            staged.at[:, pl.ds(b * block, block)],
            embedding.at[:, pl.ds(b * block, block)],
            out_sem.at[b],
        )
        write.start()
        writes.append(write)
    for write in writes:
        write.wait()


def embed(packed, start_basis, scaled):
    count, rows_here = scaled.shape
    kept = start_basis.shape[1]
    block = BLOCK
    blocks = rows_here // block
    return pl.pallas_call(
        embed_kernel,
        out_shape=(
            jax.ShapeDtypeStruct((kept, rows_here), jnp.float32),
            jax.ShapeDtypeStruct((count, kept), jnp.float32),
        ),
        in_specs=[
            pl.BlockSpec(memory_space=pltpu.VMEM),
            pl.BlockSpec(memory_space=pltpu.VMEM),
            pl.BlockSpec(memory_space=pl.ANY),
        ],
        out_specs=(
            pl.BlockSpec(memory_space=pl.ANY),
            pl.BlockSpec(memory_space=pltpu.VMEM),
        ),
        scratch_shapes=[
            pltpu.VMEM((count, count), jnp.float32),
            pltpu.VMEM((blocks, count, block), jnp.bfloat16),
            pltpu.VMEM((kept, rows_here), jnp.float32),
            pltpu.SemaphoreType.DMA((blocks,)),
            pltpu.SemaphoreType.DMA((blocks,)),
        ],
        compiler_params=pltpu.CompilerParams(vmem_limit_bytes=48 * 2**20),
    )(packed, start_basis, scaled)


def total_over(values, axes, devices):
    rows = values.shape[0] // devices
    pieces = values.reshape(devices, rows, LANES)
    pieces = lax.all_to_all(pieces, axes, 0, 0, tiled=True)
    mine = jnp.sum(pieces, axis=0)
    spread = jnp.broadcast_to(mine[None], pieces.shape)
    spread = lax.all_to_all(spread, axes, 0, 0, tiled=True)
    return spread.reshape(values.shape)


def per_device(devices, windows, landmark_index, start_basis):
    axes = ("rows", "sub")
    rows_here = windows.shape[0]
    shifted = landmark_index - lax.axis_index(axes) * rows_here
    marks = total_over(pick(shifted, windows), axes, devices)
    scaled, packed = main_pass(marks, windows, devices * CHUNK)
    packed = total_over(packed, axes, devices)
    return embed(packed, start_basis, scaled)


def solution(mesh):
    placed = (P(("rows", "sub"), None), P(), P())
    devices = int(np.prod(list(mesh.shape.values())))
    return jax.shard_map(
        functools.partial(per_device, devices),
        mesh=mesh,
        in_specs=placed,
        out_specs=(P(None, ("rows", "sub")), P()),
        check_vma=False,
    )
```

```python
import functools

import jax
import jax.numpy as jnp
import numpy as np
from jax import lax
from jax.experimental import pallas as pl
from jax.experimental.pallas import tpu as pltpu
from jax.sharding import PartitionSpec as P

ITERS = 8
BLOCK = 2048
SUB = 512
LANES = 128
CHUNK = 16

sharpness = 6.0
epsilon = 1e-06
LOG2E = 1.4426950408889634
HIGHEST = lax.Precision.HIGHEST


def dot(a, b, dims, precision=None):
    return lax.dot_general(
        a, b, (dims, ((), ())), precision=precision, preferred_element_type=jnp.float32
    )


NN = ((1,), (0,))
NT = ((1,), (1,))


def pick_kernel(axes, index, windows, out, held, listed, sem):
    count = index.shape[0]
    rows_here, width = windows.shape
    parts = width // LANES
    offset = lax.axis_index(axes) * rows_here

    def note(j, found):
        local = index[j] - offset
        listed[found] = j
        return found + ((local >= 0) & (local < rows_here)).astype(jnp.int32)

    found = lax.fori_loop(0, count, note, 0, unroll=16)

    def block_copy(n):
        start = pl.multiple_of(((index[listed[n]] - offset) // 16) * 16, 16)
        return pltpu.make_async_copy(windows.at[pl.ds(start, 16), :], held.at[n], sem)

    def begin(n, carry):
        block_copy(n).start()
        return carry

    def finish(n, carry):
        block_copy(n).wait()
        return carry

    def place(n, carry):
        j = listed[n]
        block = held[n].astype(jnp.float32)
        row = lax.broadcasted_iota(jnp.int32, block.shape, 0)
        here = row == (index[j] - offset) % 16
        row = jnp.sum(jnp.where(here, block, 0.0), axis=0, keepdims=True)
        for c in range(parts):
            out[pl.ds(parts * j + c, 1), :] = row[:, c * LANES : (c + 1) * LANES]
        return carry

    lax.fori_loop(0, found, begin, 0)
    out[...] = jnp.zeros_like(out)
    lax.fori_loop(0, found, finish, 0)
    lax.fori_loop(0, found, place, 0)


def pick(index, windows, axes):
    count, width = index.shape[0], windows.shape[1]
    return pl.pallas_call(
        functools.partial(pick_kernel, axes),
        out_shape=jax.ShapeDtypeStruct((count * width // LANES, LANES), jnp.float32),
        in_specs=[
            pl.BlockSpec(memory_space=pltpu.SMEM),
            pl.BlockSpec(memory_space=pl.ANY),
        ],
        out_specs=pl.BlockSpec(memory_space=pltpu.VMEM),
        scratch_shapes=[
            pltpu.VMEM((count, 16, width), jnp.bfloat16),
            pltpu.SMEM((count + 1,), jnp.int32),
            pltpu.SemaphoreType.DMA,
        ],
        compiler_params=pltpu.CompilerParams(vmem_limit_bytes=56 * 2**20),
    )(index, windows)


def main_kernel(marks, windows, scaled, packed, land, land_scale, cross, column):
    step = pl.program_id(0)
    count, width = land.shape
    half = count // 2
    parts = width // LANES

    @pl.when(step == 0)
    def _():
        square = jnp.zeros((count, 1), jnp.float32)
        for c in range(parts):
            piece = marks[pl.ds(c, count, stride=parts), :]
            land[:, c * LANES : (c + 1) * LANES] = piece.astype(jnp.bfloat16)
            square += jnp.sum(piece * piece, axis=1, keepdims=True)
        inverse = lax.rsqrt(square / width + epsilon)
        land_scale[...] = jnp.broadcast_to(
            inverse * (sharpness * LOG2E / width), land_scale.shape
        )
        cross[...] = jnp.zeros_like(cross)
        column[...] = jnp.zeros_like(column)

    for t in range(BLOCK // SUB):
        part = slice(t * SUB, (t + 1) * SUB)
        data = windows[part, :]
        products = dot(land[...], data, NT)
        wide = data.astype(jnp.float32)
        mean = jnp.sum(wide * wide, axis=1, keepdims=True) / width
        inverse = jnp.transpose(jnp.broadcast_to(lax.rsqrt(mean + epsilon), (SUB, LANES)))[:1]
        scale = jnp.concatenate([land_scale[...]] * (SUB // LANES), axis=1)
        affinity = jnp.exp2(products * scale * inverse)
        total = jnp.sum(affinity, axis=0, keepdims=True)
        lanes = affinity[:, :LANES]
        for c in range(1, SUB // LANES):
            lanes += affinity[:, c * LANES : (c + 1) * LANES]
        column[...] += lanes
        rounded = (affinity * lax.rsqrt(total)).astype(jnp.bfloat16)
        scaled[:, part] = rounded
        low, high = rounded[:half], rounded[half:]
        cross[0] += dot(low, low, NT)
        cross[1] += dot(high, low, NT)
        cross[2] += dot(high, high, NT)

    @pl.when(step == pl.num_programs(0) - 1)
    def _():
        packed[...] = jnp.zeros_like(packed)
        at = 0
        for b in range(3):
            for c in range(half // LANES):
                packed[at : at + half, :] = cross[b, :, c * LANES : (c + 1) * LANES]
                at += half
        for c in range(count // LANES):
            turned = jnp.transpose(column[c * LANES : (c + 1) * LANES, :])
            packed[at : at + 1, :] = jnp.sum(turned, axis=0, keepdims=True)
            at += 1


def main_pass(marks, windows, total_rows):
    rows_here, width = windows.shape
    count = marks.shape[0] * LANES // width
    half = count // 2
    return pl.pallas_call(
        main_kernel,
        grid=(rows_here // BLOCK,),
        out_shape=(
            jax.ShapeDtypeStruct((count, rows_here), jnp.bfloat16),
            jax.ShapeDtypeStruct((total_rows, LANES), jnp.float32),
        ),
        in_specs=[
            pl.BlockSpec(marks.shape, lambda i: (0, 0)),
            pl.BlockSpec((BLOCK, width), lambda i: (i, 0)),
        ],
        out_specs=(
            pl.BlockSpec((count, BLOCK), lambda i: (0, i)),
            pl.BlockSpec((total_rows, LANES), lambda i: (0, 0)),
        ),
        scratch_shapes=[
            pltpu.VMEM((count, width), jnp.bfloat16),
            pltpu.VMEM((count, LANES), jnp.float32),
            pltpu.VMEM((3, half, half), jnp.float32),
            pltpu.VMEM((count, LANES), jnp.float32),
        ],
        compiler_params=pltpu.CompilerParams(
            dimension_semantics=("arbitrary",), vmem_limit_bytes=48 * 2**20
        ),
    )(marks, windows)


def inverse_cholesky(square):
    size = square.shape[0]
    row = lax.broadcasted_iota(jnp.int32, (size, 2 * size), 0)
    lane = lax.broadcasted_iota(jnp.int32, (size, 2 * size), 1)
    table = jnp.concatenate([square, jnp.zeros_like(square)], axis=1)
    table = jnp.where(lane == row + size, 1.0, table)
    done = []
    for at in range(0, size, 8):
        left = size - at
        panel = [
            jnp.broadcast_to(table[:, at + j : at + j + 1], (left, 2 * size))
            for j in range(8)
        ]
        for j in range(8):
            pivot = panel[j][j : j + 1]
            pivot_row = table[j : j + 1]
            factor = panel[j] * (1.0 / pivot)
            first = jnp.where(row[:8] > j, factor[:8], 0.0)
            factor = jnp.concatenate([first, factor[8:]], axis=0) if left > 8 else first
            done.append((pivot_row * lax.rsqrt(pivot))[:, size:])
            for q in range(j + 1, 8):
                panel[q] -= factor * panel[q][j : j + 1]
            table -= factor * pivot_row
        table = table[8:]
    return jnp.concatenate(done, axis=0)


def embed_kernel(packed, start, scaled, embedding, basis, gram, held, staged, in_sem, out_sem):
    count = gram.shape[0]
    half = count // 2
    blocks = held.shape[0]
    block = held.shape[2]
    reads = [
        pltpu.make_async_copy(
            scaled.at[:, pl.ds(b * block, block)], held.at[b], in_sem.at[b]
        )
        for b in range(blocks)
    ]
    for read in reads:
        read.start()

    base = 3 * half * (half // LANES)
    degree = jnp.concatenate(
        [packed[base + c : base + c + 1, :] for c in range(count // LANES)], axis=1
    )
    across = lax.rsqrt(degree)
    down = jnp.concatenate(
        [
            jnp.transpose(
                jnp.broadcast_to(across[:, c * LANES : (c + 1) * LANES], (LANES, LANES))
            )
            for c in range(count // LANES)
        ],
        axis=0,
    )

    def corner(b):
        at = b * half * (half // LANES)
        return jnp.concatenate(
            [packed[at + c * half : at + (c + 1) * half, :] for c in range(half // LANES)],
            axis=1,
        )

    wide = jnp.concatenate([down[:, :1]] * 1, axis=1)
    low = corner(0) * wide[:half] * across[:, :half]
    side = corner(1) * wide[half:] * across[:, :half]
    high = corner(2) * wide[half:] * across[:, half:]
    gram[:half, :half] = low
    gram[half:, :half] = side
    gram[:half, half:] = jnp.transpose(side)
    gram[half:, half:] = high

    def iterate(_, turned):
        image = dot(turned, gram[...], NN, HIGHEST)
        square = dot(image, image, NT, HIGHEST)
        return dot(inverse_cholesky(square), image, NN, HIGHEST)

    turned = lax.fori_loop(0, ITERS, iterate, jnp.transpose(start[...]))
    basis[...] = turned
    weighted = (turned * across).astype(jnp.bfloat16)
    writes = []
    for b in range(blocks):
        reads[b].wait()
        staged[:, b * block : (b + 1) * block] = dot(weighted, held[b], NN)
        write = pltpu.make_async_copy(
            staged.at[:, pl.ds(b * block, block)],
            embedding.at[:, pl.ds(b * block, block)],
            out_sem.at[b],
        )
        write.start()
        writes.append(write)
    for write in writes:
        write.wait()


def embed(packed, start_basis, scaled):
    count, rows_here = scaled.shape
    kept = start_basis.shape[1]
    block = BLOCK
    blocks = rows_here // block
    return pl.pallas_call(
        embed_kernel,
        out_shape=(
            jax.ShapeDtypeStruct((kept, rows_here), jnp.float32),
            jax.ShapeDtypeStruct((kept, count), jnp.float32),
        ),
        in_specs=[
            pl.BlockSpec(memory_space=pltpu.VMEM),
            pl.BlockSpec(memory_space=pltpu.VMEM),
            pl.BlockSpec(memory_space=pl.ANY),
        ],
        out_specs=(
            pl.BlockSpec(memory_space=pl.ANY),
            pl.BlockSpec(memory_space=pltpu.VMEM),
        ),
        scratch_shapes=[
            pltpu.VMEM((count, count), jnp.float32),
            pltpu.VMEM((blocks, count, block), jnp.bfloat16),
            pltpu.VMEM((kept, rows_here), jnp.float32),
            pltpu.SemaphoreType.DMA((blocks,)),
            pltpu.SemaphoreType.DMA((blocks,)),
        ],
        compiler_params=pltpu.CompilerParams(vmem_limit_bytes=48 * 2**20),
    )(packed, start_basis, scaled)


def total_over(values, axes, devices):
    rows = values.shape[0] // devices
    pieces = values.reshape(devices, rows, LANES)
    pieces = lax.all_to_all(pieces, axes, 0, 0, tiled=True)
    mine = jnp.sum(pieces, axis=0)
    spread = jnp.broadcast_to(mine[None], pieces.shape)
    spread = lax.all_to_all(spread, axes, 0, 0, tiled=True)
    return spread.reshape(values.shape)


def per_device(devices, windows, landmark_index, start_basis):
    axes = ("rows", "sub")
    marks = total_over(pick(landmark_index, windows, axes), axes, devices)
    scaled, packed = main_pass(marks, windows, devices * CHUNK)
    packed = total_over(packed, axes, devices)
    embedding, turned = embed(packed, start_basis, scaled)
    return embedding, turned.T


def solution(mesh):
    placed = (P(("rows", "sub"), None), P(), P())
    devices = int(np.prod(list(mesh.shape.values())))
    return jax.shard_map(
        functools.partial(per_device, devices),
        mesh=mesh,
        in_specs=placed,
        out_specs=(P(None, ("rows", "sub")), P()),
        check_vma=False,
    )
```

```python
import functools

import jax
import jax.numpy as jnp
import numpy as np
from jax import lax
from jax.experimental import pallas as pl
from jax.experimental.pallas import tpu as pltpu
from jax.sharding import PartitionSpec as P

ITERS = 8
GROUPS = ((2, 4e-6), (3, 4e-6), (3, 2e-2))
SUB = 512
UNROLL = 4
ROWS = 16
LANES = 128
CHUNK = 16

sharpness = 6.0
epsilon = 1e-06
LOG2E = 1.4426950408889634
HIGHEST = lax.Precision.HIGHEST


def dot(a, b, dims, precision=None):
    return lax.dot_general(
        a, b, (dims, ((), ())), precision=precision, preferred_element_type=jnp.float32
    )


NN = ((1,), (0,))
NT = ((1,), (1,))


def pick_kernel(axes, index, windows, out, held, listed, sem):
    count = index.shape[0]
    rows_here, width = windows.shape
    parts = width // LANES
    offset = lax.axis_index(axes) * rows_here

    def note(j, found):
        local = index[j] - offset
        listed[found] = j
        return found + ((local >= 0) & (local < rows_here)).astype(jnp.int32)

    found = lax.fori_loop(0, count, note, 0, unroll=16)

    def block_copy(n):
        start = pl.multiple_of(((index[listed[n]] - offset) // 16) * 16, 16)
        return pltpu.make_async_copy(windows.at[pl.ds(start, 16), :], held.at[n], sem)

    def begin(n, carry):
        block_copy(n).start()
        return carry

    def finish(n, carry):
        block_copy(n).wait()
        return carry

    def place(n, carry):
        j = listed[n]
        block = held[n].astype(jnp.float32)
        row = lax.broadcasted_iota(jnp.int32, block.shape, 0)
        here = row == (index[j] - offset) % 16
        row = jnp.sum(jnp.where(here, block, 0.0), axis=0, keepdims=True)
        for c in range(parts):
            out[pl.ds(parts * j + c, 1), :] = row[:, c * LANES : (c + 1) * LANES]
        return carry

    lax.fori_loop(0, found, begin, 0)
    out[...] = jnp.zeros_like(out)
    lax.fori_loop(0, found, finish, 0)
    lax.fori_loop(0, found, place, 0)


def pick(index, windows, axes):
    count, width = index.shape[0], windows.shape[1]
    return pl.pallas_call(
        functools.partial(pick_kernel, axes),
        out_shape=jax.ShapeDtypeStruct((count * width // LANES, LANES), jnp.float32),
        in_specs=[
            pl.BlockSpec(memory_space=pltpu.SMEM),
            pl.BlockSpec(memory_space=pl.ANY),
        ],
        out_specs=pl.BlockSpec(memory_space=pltpu.VMEM),
        scratch_shapes=[
            pltpu.VMEM((count, 16, width), jnp.bfloat16),
            pltpu.SMEM((count + 1,), jnp.int32),
            pltpu.SemaphoreType.DMA,
        ],
        compiler_params=pltpu.CompilerParams(vmem_limit_bytes=56 * 2**20),
    )(index, windows)


def main_kernel(
    marks, windows, scaled, packed, land, land_scale, held, made, products, cross, column, in_sem, out_sem
):
    count, width = land.shape
    half = count // 2
    parts = width // LANES
    blocks = held.shape[0]

    def read(b):
        return pltpu.make_async_copy(
            windows.at[pl.ds(b * SUB, SUB), :], held.at[b], in_sem.at[b]
        )

    def write(b):
        return pltpu.make_async_copy(made.at[b + 1], scaled.at[b], out_sem.at[b])

    def begin(b, carry):
        read(b).start()
        return carry

    lax.fori_loop(0, blocks, begin, 0)

    square = jnp.zeros((count, 1), jnp.float32)
    for c in range(parts):
        piece = marks[pl.ds(c, count, stride=parts), :]
        land[:, c * LANES : (c + 1) * LANES] = piece.astype(jnp.bfloat16)
        square += jnp.sum(piece * piece, axis=1, keepdims=True)
    inverse = lax.rsqrt(square / width + epsilon)
    land_scale[...] = jnp.broadcast_to(
        inverse * (sharpness * LOG2E / width), land_scale.shape
    )
    cross[...] = jnp.zeros_like(cross)
    column[...] = jnp.zeros_like(column)
    made[0] = jnp.zeros(made.shape[1:], made.dtype)

    def multiply(b, slot):
        products[slot] = dot(land[...], held[b], NT)

    def window_scale(b):
        lane = lax.broadcasted_iota(jnp.int32, (LANES, LANES), 1)
        table = jnp.zeros((LANES, LANES), jnp.float32)
        for g in range(SUB // LANES):
            wide = held[b, g * LANES : (g + 1) * LANES, :].astype(jnp.float32)
            wide = wide * wide
            lanes = wide[:, :LANES]
            for c in range(1, parts):
                lanes += wide[:, c * LANES : (c + 1) * LANES]
            mean = jnp.sum(lanes, axis=1, keepdims=True) / width
            table = jnp.where(lane == g, mean, table)
        table = jnp.transpose(table)[: SUB // LANES]
        table = lax.rsqrt(table + epsilon)
        return jnp.concatenate([table[g : g + 1] for g in range(SUB // LANES)], axis=1)

    def shape(b, slot):
        inverse = jnp.broadcast_to(window_scale(b), (ROWS, SUB))
        total = jnp.zeros((8, SUB), jnp.float32)
        for r in range(0, count, ROWS):
            scale = jnp.concatenate([land_scale[r : r + ROWS, :]] * (SUB // LANES), axis=1)
            affinity = jnp.exp2(products[slot, r : r + ROWS, :] * scale * inverse)
            products[slot, r : r + ROWS, :] = affinity
            for k in range(0, ROWS, 8):
                total += affinity[k : k + 8]
            lanes = affinity[:, :LANES]
            for c in range(1, SUB // LANES):
                lanes += affinity[:, c * LANES : (c + 1) * LANES]
            column[r : r + ROWS, :] += lanes
        root = lax.rsqrt(jnp.sum(total, axis=0, keepdims=True))
        root = jnp.broadcast_to(root, (ROWS, SUB))
        for r in range(0, count, ROWS):
            made[b + 1, r : r + ROWS, :] = (products[slot, r : r + ROWS, :] * root).astype(
                jnp.bfloat16
            )

    def gather(b):
        low, high = made[b + 1, :half], made[b + 1, half:]
        cross[0] += dot(low, low, NT)
        cross[1] += dot(high, low, NT)
        cross[2] += dot(high, high, NT)

    read(0).wait()
    multiply(0, 0)

    def several(i, carry):
        b = UNROLL * i
        for k in range(1, UNROLL):
            read(b + k).wait()

        @pl.when(b + UNROLL < blocks)
        def _():
            read(b + UNROLL).wait()

        for k in range(UNROLL):
            following = b + k + 1 if k + 1 < UNROLL else jnp.minimum(b + UNROLL, blocks - 1)
            gather(b + k - 1)
            multiply(following, (k + 1) % 2)
            shape(b + k, k % 2)
        for k in range(UNROLL):
            write(b + k).start()
        return carry

    lax.fori_loop(0, blocks // UNROLL, several, 0)
    gather(blocks - 1)

    packed[...] = jnp.zeros_like(packed)
    at = 0
    for b in range(3):
        for c in range(half // LANES):
            packed[at : at + half, :] = cross[b, :, c * LANES : (c + 1) * LANES]
            at += half
    for c in range(count // LANES):
        turned = jnp.transpose(column[c * LANES : (c + 1) * LANES, :])
        packed[at : at + 1, :] = jnp.sum(turned, axis=0, keepdims=True)
        at += 1

    def finish(b, carry):
        write(b).wait()
        return carry

    lax.fori_loop(0, blocks, finish, 0)


def main_pass(marks, windows, total_rows):
    rows_here, width = windows.shape
    count = marks.shape[0] * LANES // width
    half = count // 2
    blocks = rows_here // SUB
    return pl.pallas_call(
        main_kernel,
        out_shape=(
            jax.ShapeDtypeStruct((blocks, count, SUB), jnp.bfloat16),
            jax.ShapeDtypeStruct((total_rows, LANES), jnp.float32),
        ),
        in_specs=[
            pl.BlockSpec(memory_space=pltpu.VMEM),
            pl.BlockSpec(memory_space=pl.ANY),
        ],
        out_specs=(
            pl.BlockSpec(memory_space=pl.ANY),
            pl.BlockSpec(memory_space=pltpu.VMEM),
        ),
        scratch_shapes=[
            pltpu.VMEM((count, width), jnp.bfloat16),
            pltpu.VMEM((count, LANES), jnp.float32),
            pltpu.VMEM((blocks, SUB, width), jnp.bfloat16),
            pltpu.VMEM((blocks + 1, count, SUB), jnp.bfloat16),
            pltpu.VMEM((2, count, SUB), jnp.float32),
            pltpu.VMEM((3, half, half), jnp.float32),
            pltpu.VMEM((count, LANES), jnp.float32),
            pltpu.SemaphoreType.DMA((blocks,)),
            pltpu.SemaphoreType.DMA((blocks,)),
        ],
        compiler_params=pltpu.CompilerParams(vmem_limit_bytes=44 * 2**20),
    )(marks, windows)


def split(values):
    high = values.astype(jnp.bfloat16)
    rest = values - high.astype(jnp.float32)
    middle = rest.astype(jnp.bfloat16)
    low = (rest - middle.astype(jnp.float32)).astype(jnp.bfloat16)
    return high, middle, low


def exact_dot(a, b, dims):
    n = a[0].shape[0]
    high = dot(jnp.concatenate(a, axis=0), b[0], dims)
    middle = dot(jnp.concatenate(a[:2], axis=0), b[1], dims)
    low = dot(a[0], b[2], dims)
    small = high[2 * n :] + middle[n:] + low
    return high[:n] + (high[n : 2 * n] + middle[:n] + small)


def inverse_cholesky(square):
    size = square.shape[0]
    row = lax.broadcasted_iota(jnp.int32, (size, 2 * size), 0)
    lane = lax.broadcasted_iota(jnp.int32, (size, 2 * size), 1)
    table = jnp.concatenate([square, jnp.zeros_like(square)], axis=1)
    diagonal = jnp.sum(jnp.where(lane == row, table, 0.0), axis=1, keepdims=True)
    table = jnp.where(lane == row + size, 1.0, table)
    done, pivots = [], []
    for at in range(0, size, 8):
        left = size - at
        panel = [
            jnp.broadcast_to(table[:, at + j : at + j + 1], (left, 2 * size))
            for j in range(8)
        ]
        for j in range(8):
            pivot = panel[j][j : j + 1]
            pivot_row = table[j : j + 1]
            factor = panel[j] * (1.0 / pivot)
            first = jnp.where(row[:8] > j, factor[:8], 0.0)
            factor = jnp.concatenate([first, factor[8:]], axis=0) if left > 8 else first
            done.append((pivot_row * lax.rsqrt(pivot))[:, size:])
            pivots.append(pivot)
            for q in range(j + 1, 8):
                panel[q] -= factor * panel[q][j : j + 1]
            table -= factor * pivot_row
        table = table[8:]
    return jnp.concatenate(done, axis=0), jnp.concatenate(pivots, axis=0) / diagonal


def embed_kernel(packed, start, scaled, embedding, basis, gram, held, staged, turned, in_sem, out_sem):
    count = gram.shape[1]
    half = count // 2
    blocks, _, block = held.shape

    def read(b):
        return pltpu.make_async_copy(scaled.at[b], held.at[b], in_sem.at[b])

    def write(b):
        return pltpu.make_async_copy(
            staged.at[:, pl.ds(b * block, block)],
            embedding.at[:, pl.ds(b * block, block)],
            out_sem.at[b],
        )

    for b in range(blocks):
        read(b).start()

    base = 3 * half * (half // LANES)
    degree = jnp.concatenate(
        [packed[base + c : base + c + 1, :] for c in range(count // LANES)], axis=1
    )
    across = lax.rsqrt(degree)
    down = jnp.concatenate(
        [
            jnp.transpose(
                jnp.broadcast_to(across[:, c * LANES : (c + 1) * LANES], (LANES, LANES))
            )
            for c in range(count // LANES)
        ],
        axis=0,
    )

    def corner(b):
        at = b * half * (half // LANES)
        return jnp.concatenate(
            [packed[at + c * half : at + (c + 1) * half, :] for c in range(half // LANES)],
            axis=1,
        )

    def fill(rows, columns, values):
        for term, part in enumerate(split(values)):
            gram[term, rows, columns] = part

    wide = jnp.concatenate([down] * (half // LANES), axis=1)
    first, second = slice(0, half), slice(half, count)
    side = corner(1) * wide[half:] * across[:, :half]
    fill(first, first, corner(0) * wide[:half] * across[:, :half])
    fill(second, first, side)
    fill(first, second, jnp.transpose(side))
    fill(second, second, corner(2) * wide[half:] * across[:, half:])

    def advance(rows, steps):
        for _ in range(steps):
            rows = exact_dot(split(rows), [gram[0], gram[1], gram[2]], NN)
        terms = split(rows)
        inverse, ratio = inverse_cholesky(exact_dot(terms, terms, NT))
        return exact_dot(split(inverse), terms, NN), ratio

    begin = jnp.transpose(start[...])
    rows, good = begin, None
    for steps, least in GROUPS:
        rows, ratio = advance(rows, steps)
        here = jnp.where(ratio > least, 1.0, 0.0)
        good = here if good is None else good * here
    turned[...] = rows

    @pl.when(jnp.logical_not(jnp.min(good) > 0.5))
    def _():
        turned[...] = lax.fori_loop(0, ITERS, lambda _, rows: advance(rows, 1)[0], begin)

    basis[...] = turned[...]
    weighted = (turned[...] * across).astype(jnp.bfloat16)
    for b in range(blocks):
        read(b).wait()
        staged[:, b * block : (b + 1) * block] = dot(weighted, held[b], NN)
        write(b).start()
    for b in range(blocks):
        write(b).wait()


def embed(packed, start_basis, scaled):
    blocks, count, block = scaled.shape
    kept = start_basis.shape[1]
    rows_here = blocks * block
    return pl.pallas_call(
        embed_kernel,
        out_shape=(
            jax.ShapeDtypeStruct((kept, rows_here), jnp.float32),
            jax.ShapeDtypeStruct((kept, count), jnp.float32),
        ),
        in_specs=[
            pl.BlockSpec(memory_space=pltpu.VMEM),
            pl.BlockSpec(memory_space=pltpu.VMEM),
            pl.BlockSpec(memory_space=pl.ANY),
        ],
        out_specs=(
            pl.BlockSpec(memory_space=pl.ANY),
            pl.BlockSpec(memory_space=pltpu.VMEM),
        ),
        scratch_shapes=[
            pltpu.VMEM((3, count, count), jnp.bfloat16),
            pltpu.VMEM((blocks, count, block), jnp.bfloat16),
            pltpu.VMEM((kept, rows_here), jnp.float32),
            pltpu.VMEM((kept, count), jnp.float32),
            pltpu.SemaphoreType.DMA((blocks,)),
            pltpu.SemaphoreType.DMA((blocks,)),
        ],
        compiler_params=pltpu.CompilerParams(vmem_limit_bytes=50 * 2**20),
    )(packed, start_basis, scaled)


def total_over(values, axes, devices):
    rows = values.shape[0] // devices
    pieces = values.reshape(devices, rows, LANES)
    pieces = lax.all_to_all(pieces, axes, 0, 0, tiled=True)
    mine = jnp.sum(pieces, axis=0)
    spread = jnp.broadcast_to(mine[None], pieces.shape)
    spread = lax.all_to_all(spread, axes, 0, 0, tiled=True)
    return spread.reshape(values.shape)


def per_device(devices, windows, landmark_index, start_basis):
    axes = ("rows", "sub")
    marks = total_over(pick(landmark_index, windows, axes), axes, devices)
    scaled, packed = main_pass(marks, windows, devices * CHUNK)
    packed = total_over(packed, axes, devices)
    embedding, turned = embed(packed, start_basis, scaled)
    return embedding, turned.T


def solution(mesh):
    placed = (P(("rows", "sub"), None), P(), P())
    devices = int(np.prod(list(mesh.shape.values())))
    return jax.shard_map(
        functools.partial(per_device, devices),
        mesh=mesh,
        in_specs=placed,
        out_specs=(P(None, ("rows", "sub")), P()),
        check_vma=False,
    )
```

```python
import functools

import jax
import jax.numpy as jnp
from jax import lax
from jax.experimental import pallas as pl
from jax.experimental.pallas import tpu as pltpu
from jax.sharding import PartitionSpec as P

ITERS = 8
GROUPS = ((2, 4e-6), (3, 4e-6), (3, 2e-2))
SUB = 512
UNROLL = 4
ROWS = 16
LANES = 128
CHUNK = 16

sharpness = 6.0
epsilon = 1e-06
LOG2E = 1.4426950408889634
HIGHEST = lax.Precision.HIGHEST


def dot(a, b, dims, precision=None):
    return lax.dot_general(
        a, b, (dims, ((), ())), precision=precision, preferred_element_type=jnp.float32
    )


NN = ((1,), (0,))
NT = ((1,), (1,))


def pick_kernel(axes, index, windows, keep, send, held, listed, sem):
    count = index.shape[0]
    rows_here, width = windows.shape
    parts = width // LANES
    offset = lax.axis_index(axes) * rows_here
    core = lax.axis_index(axes[0]) % 2
    half = keep.shape[0]

    def note(j, found):
        local = index[j] - offset
        listed[found] = j
        return found + ((local >= 0) & (local < rows_here)).astype(jnp.int32)

    found = lax.fori_loop(0, count, note, 0, unroll=16)

    def block_copy(n):
        start = pl.multiple_of(((index[listed[n]] - offset) // 16) * 16, 16)
        return pltpu.make_async_copy(windows.at[pl.ds(start, 16), :], held.at[n], sem)

    def begin(n, carry):
        block_copy(n).start()
        return carry

    def finish(n, carry):
        block_copy(n).wait()
        return carry

    def place(n, carry):
        j = listed[n]
        block = held[n].astype(jnp.float32)
        row = lax.broadcasted_iota(jnp.int32, block.shape, 0)
        here = row == (index[j] - offset) % 16
        row = jnp.sum(jnp.where(here, block, 0.0), axis=0, keepdims=True)
        for side, out in ((core, keep), (1 - core, send)):

            @pl.when((parts * j) // half == side)
            def _():
                for c in range(parts):
                    out[pl.ds((parts * j) % half + c, 1), :] = row[:, c * LANES : (c + 1) * LANES]

        return carry

    lax.fori_loop(0, found, begin, 0)
    keep[...] = jnp.zeros_like(keep)
    send[...] = jnp.zeros_like(send)
    lax.fori_loop(0, found, finish, 0)
    lax.fori_loop(0, found, place, 0)


def pick(index, windows, axes):
    count, width = index.shape[0], windows.shape[1]
    return pl.pallas_call(
        functools.partial(pick_kernel, axes),
        out_shape=(
            jax.ShapeDtypeStruct((count * width // LANES // 2, LANES), jnp.float32),
        ) * 2,
        in_specs=[
            pl.BlockSpec(memory_space=pltpu.SMEM),
            pl.BlockSpec(memory_space=pl.ANY),
        ],
        out_specs=(pl.BlockSpec(memory_space=pltpu.VMEM),) * 2,
        scratch_shapes=[
            pltpu.VMEM((count, 16, width), jnp.bfloat16),
            pltpu.SMEM((count + 1,), jnp.int32),
            pltpu.SemaphoreType.DMA,
        ],
        compiler_params=pltpu.CompilerParams(vmem_limit_bytes=56 * 2**20),
    )(index, windows)


def main_kernel(
    axis, own, other, windows, scaled, keep, send, land, land_scale, held, made, products, cross, column, in_sem, out_sem
):
    core = lax.axis_index(axis) % 2
    count, width = land.shape
    half = count // 2
    parts = width // LANES
    blocks = held.shape[0]

    def read(b):
        return pltpu.make_async_copy(
            windows.at[pl.ds(b * SUB, SUB), :], held.at[b], in_sem.at[b]
        )

    def write(b):
        return pltpu.make_async_copy(made.at[b + 1], scaled.at[b], out_sem.at[b])

    def begin(b, carry):
        read(b).start()
        return carry

    lax.fori_loop(0, blocks, begin, 0)

    for side, marks in ((core, own), (1 - core, other)):
        here = pl.ds(pl.multiple_of(side * half, half), half)
        square = jnp.zeros((half, 1), jnp.float32)
        for c in range(parts):
            piece = marks[pl.ds(c, half, stride=parts), :]
            land[here, c * LANES : (c + 1) * LANES] = piece.astype(jnp.bfloat16)
            square += jnp.sum(piece * piece, axis=1, keepdims=True)
        inverse = lax.rsqrt(square / width + epsilon)
        land_scale[here, :] = jnp.broadcast_to(
            inverse * (sharpness * LOG2E / width), (half, LANES)
        )
    cross[...] = jnp.zeros_like(cross)
    column[...] = jnp.zeros_like(column)
    made[0] = jnp.zeros(made.shape[1:], made.dtype)

    def multiply(b, slot):
        products[slot] = dot(land[...], held[b], NT)

    def window_scale(b):
        lane = lax.broadcasted_iota(jnp.int32, (LANES, LANES), 1)
        table = jnp.zeros((LANES, LANES), jnp.float32)
        for g in range(SUB // LANES):
            wide = held[b, g * LANES : (g + 1) * LANES, :].astype(jnp.float32)
            wide = wide * wide
            lanes = wide[:, :LANES]
            for c in range(1, parts):
                lanes += wide[:, c * LANES : (c + 1) * LANES]
            mean = jnp.sum(lanes, axis=1, keepdims=True) / width
            table = jnp.where(lane == g, mean, table)
        table = jnp.transpose(table)[: SUB // LANES]
        table = lax.rsqrt(table + epsilon)
        return jnp.concatenate([table[g : g + 1] for g in range(SUB // LANES)], axis=1)

    def shape(b, slot):
        inverse = jnp.broadcast_to(window_scale(b), (ROWS, SUB))
        total = jnp.zeros((8, SUB), jnp.float32)
        for r in range(0, count, ROWS):
            scale = jnp.concatenate([land_scale[r : r + ROWS, :]] * (SUB // LANES), axis=1)
            affinity = jnp.exp2(products[slot, r : r + ROWS, :] * scale * inverse)
            products[slot, r : r + ROWS, :] = affinity
            for k in range(0, ROWS, 8):
                total += affinity[k : k + 8]
            lanes = affinity[:, :LANES]
            for c in range(1, SUB // LANES):
                lanes += affinity[:, c * LANES : (c + 1) * LANES]
            column[r : r + ROWS, :] += lanes
        root = lax.rsqrt(jnp.sum(total, axis=0, keepdims=True))
        root = jnp.broadcast_to(root, (ROWS, SUB))
        for r in range(0, count, ROWS):
            made[b + 1, r : r + ROWS, :] = (products[slot, r : r + ROWS, :] * root).astype(
                jnp.bfloat16
            )

    def gather(b):
        low, high = made[b + 1, :half], made[b + 1, half:]
        cross[0] += dot(low, low, NT)
        cross[1] += dot(high, low, NT)
        cross[2] += dot(high, high, NT)

    read(0).wait()
    multiply(0, 0)

    def several(i, carry):
        b = UNROLL * i
        for k in range(1, UNROLL):
            read(b + k).wait()

        @pl.when(b + UNROLL < blocks)
        def _():
            read(b + UNROLL).wait()

        for k in range(UNROLL):
            following = b + k + 1 if k + 1 < UNROLL else jnp.minimum(b + UNROLL, blocks - 1)
            gather(b + k - 1)
            multiply(following, (k + 1) % 2)
            shape(b + k, k % 2)
        for k in range(UNROLL):
            write(b + k).start()
        return carry

    lax.fori_loop(0, blocks // UNROLL, several, 0)
    gather(blocks - 1)

    keep[...] = jnp.zeros_like(keep)
    send[...] = jnp.zeros_like(send)

    def place(at, values):
        which, row = divmod(at, keep.shape[0])
        for side, out in ((core, keep), (1 - core, send)):

            @pl.when(side == which)
            def _():
                out[row : row + values.shape[0], :] = values

    at = 0
    for b in range(3):
        for c in range(half // LANES):
            place(at, cross[b, :, c * LANES : (c + 1) * LANES])
            at += half
    degrees = []
    for c in range(count // LANES):
        turned = jnp.transpose(column[c * LANES : (c + 1) * LANES, :])
        degrees.append(jnp.sum(turned, axis=0, keepdims=True))
    place(at, jnp.concatenate(degrees, axis=0))

    def finish(b, carry):
        write(b).wait()
        return carry

    lax.fori_loop(0, blocks, finish, 0)


def main_pass(own, other, windows, total_rows, axis):
    rows_here, width = windows.shape
    count = 2 * own.shape[0] * LANES // width
    half = count // 2
    blocks = rows_here // SUB
    return pl.pallas_call(
        functools.partial(main_kernel, axis),
        out_shape=(
            jax.ShapeDtypeStruct((blocks, count, SUB), jnp.bfloat16),
            jax.ShapeDtypeStruct((total_rows // 2, LANES), jnp.float32),
            jax.ShapeDtypeStruct((total_rows // 2, LANES), jnp.float32),
        ),
        in_specs=[
            pl.BlockSpec(memory_space=pltpu.VMEM),
            pl.BlockSpec(memory_space=pltpu.VMEM),
            pl.BlockSpec(memory_space=pl.ANY),
        ],
        out_specs=(
            pl.BlockSpec(memory_space=pl.ANY),
            pl.BlockSpec(memory_space=pltpu.VMEM),
            pl.BlockSpec(memory_space=pltpu.VMEM),
        ),
        scratch_shapes=[
            pltpu.VMEM((count, width), jnp.bfloat16),
            pltpu.VMEM((count, LANES), jnp.float32),
            pltpu.VMEM((blocks, SUB, width), jnp.bfloat16),
            pltpu.VMEM((blocks + 1, count, SUB), jnp.bfloat16),
            pltpu.VMEM((2, count, SUB), jnp.float32),
            pltpu.VMEM((3, half, half), jnp.float32),
            pltpu.VMEM((count, LANES), jnp.float32),
            pltpu.SemaphoreType.DMA((blocks,)),
            pltpu.SemaphoreType.DMA((blocks,)),
        ],
        compiler_params=pltpu.CompilerParams(vmem_limit_bytes=44 * 2**20),
    )(own, other, windows)


def split(values):
    high = values.astype(jnp.bfloat16)
    rest = values - high.astype(jnp.float32)
    middle = rest.astype(jnp.bfloat16)
    low = (rest - middle.astype(jnp.float32)).astype(jnp.bfloat16)
    return high, middle, low


def exact_dot(a, b, dims):
    n = a[0].shape[0]
    high = dot(jnp.concatenate(a, axis=0), b[0], dims)
    middle = dot(jnp.concatenate(a[:2], axis=0), b[1], dims)
    low = dot(a[0], b[2], dims)
    small = high[2 * n :] + middle[n:] + low
    return high[:n] + (high[n : 2 * n] + middle[:n] + small)


def inverse_cholesky(square):
    size = square.shape[0]
    row = lax.broadcasted_iota(jnp.int32, (size, 2 * size), 0)
    lane = lax.broadcasted_iota(jnp.int32, (size, 2 * size), 1)
    table = jnp.concatenate([square, jnp.zeros_like(square)], axis=1)
    diagonal = jnp.sum(jnp.where(lane == row, table, 0.0), axis=1, keepdims=True)
    table = jnp.where(lane == row + size, 1.0, table)
    done, pivots = [], []
    for at in range(0, size, 8):
        left = size - at
        panel = [
            jnp.broadcast_to(table[:, at + j : at + j + 1], (left, 2 * size))
            for j in range(8)
        ]
        for j in range(8):
            pivot = panel[j][j : j + 1]
            pivot_row = table[j : j + 1]
            factor = panel[j] * (1.0 / pivot)
            first = jnp.where(row[:8] > j, factor[:8], 0.0)
            factor = jnp.concatenate([first, factor[8:]], axis=0) if left > 8 else first
            done.append((pivot_row * lax.rsqrt(pivot))[:, size:])
            pivots.append(pivot)
            for q in range(j + 1, 8):
                panel[q] -= factor * panel[q][j : j + 1]
            table -= factor * pivot_row
        table = table[8:]
    return jnp.concatenate(done, axis=0), jnp.concatenate(pivots, axis=0) / diagonal


def embed_kernel(
    axis, own, other, start, scaled, embedding, basis, packed, gram, held, staged, turned, in_sem, out_sem
):
    core = lax.axis_index(axis) % 2
    count = gram.shape[1]
    half = count // 2
    blocks, _, block = held.shape

    def read(b):
        return pltpu.make_async_copy(scaled.at[b], held.at[b], in_sem.at[b])

    def write(b):
        return pltpu.make_async_copy(
            staged.at[:, pl.ds(b * block, block)],
            embedding.at[:, pl.ds(b * block, block)],
            out_sem.at[b],
        )

    for b in range(blocks):
        read(b).start()

    size = own.shape[0]
    packed[pl.ds(pl.multiple_of(core * size, size), size), :] = own[...]
    packed[pl.ds(pl.multiple_of((1 - core) * size, size), size), :] = other[...]
    base = 3 * half * (half // LANES)
    degree = jnp.concatenate(
        [packed[base + c : base + c + 1, :] for c in range(count // LANES)], axis=1
    )
    across = lax.rsqrt(degree)
    down = jnp.concatenate(
        [
            jnp.transpose(
                jnp.broadcast_to(across[:, c * LANES : (c + 1) * LANES], (LANES, LANES))
            )
            for c in range(count // LANES)
        ],
        axis=0,
    )

    def corner(b):
        at = b * half * (half // LANES)
        return jnp.concatenate(
            [packed[at + c * half : at + (c + 1) * half, :] for c in range(half // LANES)],
            axis=1,
        )

    def fill(rows, columns, values):
        for term, part in enumerate(split(values)):
            gram[term, rows, columns] = part

    wide = jnp.concatenate([down] * (half // LANES), axis=1)
    first, second = slice(0, half), slice(half, count)
    side = corner(1) * wide[half:] * across[:, :half]
    fill(first, first, corner(0) * wide[:half] * across[:, :half])
    fill(second, first, side)
    fill(first, second, jnp.transpose(side))
    fill(second, second, corner(2) * wide[half:] * across[:, half:])

    def advance(rows, steps):
        for _ in range(steps):
            rows = exact_dot(split(rows), [gram[0], gram[1], gram[2]], NN)
        terms = split(rows)
        inverse, ratio = inverse_cholesky(exact_dot(terms, terms, NT))
        return exact_dot(split(inverse), terms, NN), ratio

    begin = jnp.transpose(start[...])
    rows, good = begin, None
    for steps, least in GROUPS:
        rows, ratio = advance(rows, steps)
        here = jnp.where(ratio > least, 1.0, 0.0)
        good = here if good is None else good * here
    turned[...] = rows

    @pl.when(jnp.logical_not(jnp.min(good) > 0.5))
    def _():
        turned[...] = lax.fori_loop(0, ITERS, lambda _, rows: advance(rows, 1)[0], begin)

    basis[...] = turned[...]
    weighted = (turned[...] * across).astype(jnp.bfloat16)
    for b in range(blocks):
        read(b).wait()
        staged[:, b * block : (b + 1) * block] = dot(weighted, held[b], NN)
        write(b).start()
    for b in range(blocks):
        write(b).wait()


def embed(own, other, start_basis, scaled, axis):
    blocks, count, block = scaled.shape
    kept = start_basis.shape[1]
    rows_here = blocks * block
    return pl.pallas_call(
        functools.partial(embed_kernel, axis),
        out_shape=(
            jax.ShapeDtypeStruct((kept, rows_here), jnp.float32),
            jax.ShapeDtypeStruct((kept, count), jnp.float32),
        ),
        in_specs=[
            pl.BlockSpec(memory_space=pltpu.VMEM),
            pl.BlockSpec(memory_space=pltpu.VMEM),
            pl.BlockSpec(memory_space=pltpu.VMEM),
            pl.BlockSpec(memory_space=pl.ANY),
        ],
        out_specs=(
            pl.BlockSpec(memory_space=pl.ANY),
            pl.BlockSpec(memory_space=pltpu.VMEM),
        ),
        scratch_shapes=[
            pltpu.VMEM((2 * own.shape[0], LANES), jnp.float32),
            pltpu.VMEM((3, count, count), jnp.bfloat16),
            pltpu.VMEM((blocks, count, block), jnp.bfloat16),
            pltpu.VMEM((kept, rows_here), jnp.float32),
            pltpu.VMEM((kept, count), jnp.float32),
            pltpu.SemaphoreType.DMA((blocks,)),
            pltpu.SemaphoreType.DMA((blocks,)),
        ],
        compiler_params=pltpu.CompilerParams(vmem_limit_bytes=50 * 2**20),
    )(own, other, start_basis, scaled)


def total_over(keep, send, axes, shape):
    rows, sub = shape
    chips = rows // 2 * sub
    cores = [(r, r ^ 1) for r in range(rows)]
    groups = [
        [r * sub + s for r in range(c, rows, 2) for s in range(sub)] for c in range(2)
    ]

    def exchange(values):
        return lax.all_to_all(
            values, axes, 0, 0, axis_index_groups=groups, tiled=True
        )

    values = keep + lax.ppermute(send, axes[0], cores)
    pieces = exchange(values.reshape(chips, keep.shape[0] // chips, LANES))
    mine = jnp.sum(pieces, axis=0)
    own = exchange(jnp.broadcast_to(mine[None], pieces.shape)).reshape(keep.shape)
    return own, lax.ppermute(own, axes[0], cores)


def per_device(shape, windows, landmark_index, start_basis):
    axes = ("rows", "sub")
    own, other = total_over(*pick(landmark_index, windows, axes), axes, shape)
    total_rows = shape[0] * shape[1] * CHUNK
    scaled, keep, send = main_pass(own, other, windows, total_rows, axes[0])
    own, other = total_over(keep, send, axes, shape)
    embedding, turned = embed(own, other, start_basis, scaled, axes[0])
    return embedding, turned.T


def solution(mesh):
    placed = (P(("rows", "sub"), None), P(), P())
    shape = (mesh.shape["rows"], mesh.shape["sub"])
    return jax.shard_map(
        functools.partial(per_device, shape),
        mesh=mesh,
        in_specs=placed,
        out_specs=(P(None, ("rows", "sub")), P()),
        check_vma=False,
    )
```

```python
import functools

import jax
import jax.numpy as jnp
from jax import lax
from jax.experimental import pallas as pl
from jax.experimental.pallas import tpu as pltpu
from jax.sharding import PartitionSpec as P

ITERS = 8
GROUPS = ((2, 4e-6), (3, 4e-6), (3, 2e-2))
SUB = 512
UNROLL = 4
ROWS = 16
LANES = 128
CHUNK = 16

sharpness = 6.0
epsilon = 1e-06
LOG2E = 1.4426950408889634
HIGHEST = lax.Precision.HIGHEST


def dot(a, b, dims, precision=None):
    return lax.dot_general(
        a, b, (dims, ((), ())), precision=precision, preferred_element_type=jnp.float32
    )


NN = ((1,), (0,))
NT = ((1,), (1,))


def pick_kernel(axes, index, windows, keep, send, held, listed, sem):
    count = index.shape[0]
    rows_here, width = windows.shape
    parts = width // LANES
    offset = lax.axis_index(axes) * rows_here
    core = lax.axis_index(axes[0]) % 2
    half = keep.shape[0]

    def note(j, found):
        local = index[j] - offset
        listed[found] = j
        return found + ((local >= 0) & (local < rows_here)).astype(jnp.int32)

    found = lax.fori_loop(0, count, note, 0, unroll=16)

    def block_copy(n):
        start = pl.multiple_of(((index[listed[n]] - offset) // 16) * 16, 16)
        return pltpu.make_async_copy(windows.at[pl.ds(start, 16), :], held.at[n], sem)

    def begin(n, carry):
        block_copy(n).start()
        return carry

    def finish(n, carry):
        block_copy(n).wait()
        return carry

    def place(n, carry):
        j = listed[n]
        block = held[n].astype(jnp.float32)
        row = lax.broadcasted_iota(jnp.int32, block.shape, 0)
        here = row == (index[j] - offset) % 16
        row = jnp.sum(jnp.where(here, block, 0.0), axis=0, keepdims=True)
        for side, out in ((core, keep), (1 - core, send)):

            @pl.when((parts * j) // half == side)
            def _():
                for c in range(parts):
                    out[pl.ds((parts * j) % half + c, 1), :] = row[:, c * LANES : (c + 1) * LANES]

        return carry

    lax.fori_loop(0, found, begin, 0)
    keep[...] = jnp.zeros_like(keep)
    send[...] = jnp.zeros_like(send)
    lax.fori_loop(0, found, finish, 0)
    lax.fori_loop(0, found, place, 0)


def pick(index, windows, axes):
    count, width = index.shape[0], windows.shape[1]
    return pl.pallas_call(
        functools.partial(pick_kernel, axes),
        out_shape=(
            jax.ShapeDtypeStruct((count * width // LANES // 2, LANES), jnp.float32),
        ) * 2,
        in_specs=[
            pl.BlockSpec(memory_space=pltpu.SMEM),
            pl.BlockSpec(memory_space=pl.ANY),
        ],
        out_specs=(pl.BlockSpec(memory_space=pltpu.VMEM),) * 2,
        scratch_shapes=[
            pltpu.VMEM((count, 16, width), jnp.bfloat16),
            pltpu.SMEM((count + 1,), jnp.int32),
            pltpu.SemaphoreType.DMA,
        ],
        compiler_params=pltpu.CompilerParams(vmem_limit_bytes=44 * 2**20),
    )(index, windows)


def main_kernel(
    axis, own, other, windows, scaled, keep, send, land, land_scale, held, made, products, cross, column, in_sem, out_sem
):
    core = lax.axis_index(axis) % 2
    count, width = land.shape
    half = count // 2
    parts = width // LANES
    blocks = held.shape[0]

    def read(b):
        return pltpu.make_async_copy(
            windows.at[pl.ds(b * SUB, SUB), :], held.at[b], in_sem.at[b]
        )

    def write(b):
        return pltpu.make_async_copy(made.at[b + 1], scaled.at[b], out_sem.at[b])

    def begin(b, carry):
        read(b).start()
        return carry

    lax.fori_loop(0, blocks, begin, 0)

    for side, marks in ((core, own), (1 - core, other)):
        here = pl.ds(pl.multiple_of(side * half, half), half)
        square = jnp.zeros((half, 1), jnp.float32)
        for c in range(parts):
            piece = marks[pl.ds(c, half, stride=parts), :]
            land[here, c * LANES : (c + 1) * LANES] = piece.astype(jnp.bfloat16)
            square += jnp.sum(piece * piece, axis=1, keepdims=True)
        inverse = lax.rsqrt(square / width + epsilon)
        land_scale[here, :] = jnp.broadcast_to(
            inverse * (sharpness * LOG2E / width), (half, LANES)
        )
    cross[...] = jnp.zeros_like(cross)
    column[...] = jnp.zeros_like(column)
    made[0] = jnp.zeros(made.shape[1:], made.dtype)

    def multiply(b, slot):
        products[slot] = dot(land[...], held[b], NT)

    def window_scale(b):
        lane = lax.broadcasted_iota(jnp.int32, (LANES, LANES), 1)
        table = jnp.zeros((LANES, LANES), jnp.float32)
        for g in range(SUB // LANES):
            wide = held[b, g * LANES : (g + 1) * LANES, :].astype(jnp.float32)
            wide = wide * wide
            lanes = wide[:, :LANES]
            for c in range(1, parts):
                lanes += wide[:, c * LANES : (c + 1) * LANES]
            mean = jnp.sum(lanes, axis=1, keepdims=True) / width
            table = jnp.where(lane == g, mean, table)
        table = jnp.transpose(table)[: SUB // LANES]
        table = lax.rsqrt(table + epsilon)
        return jnp.concatenate([table[g : g + 1] for g in range(SUB // LANES)], axis=1)

    def shape(b, slot):
        inverse = jnp.broadcast_to(window_scale(b), (ROWS, SUB))
        total = jnp.zeros((8, SUB), jnp.float32)
        for r in range(0, count, ROWS):
            scale = jnp.concatenate([land_scale[r : r + ROWS, :]] * (SUB // LANES), axis=1)
            affinity = jnp.exp2(products[slot, r : r + ROWS, :] * scale * inverse)
            products[slot, r : r + ROWS, :] = affinity
            for k in range(0, ROWS, 8):
                total += affinity[k : k + 8]
            lanes = affinity[:, :LANES]
            for c in range(1, SUB // LANES):
                lanes += affinity[:, c * LANES : (c + 1) * LANES]
            column[r : r + ROWS, :] += lanes
        root = lax.rsqrt(jnp.sum(total, axis=0, keepdims=True))
        root = jnp.broadcast_to(root, (ROWS, SUB))
        for r in range(0, count, ROWS):
            made[b + 1, r : r + ROWS, :] = (products[slot, r : r + ROWS, :] * root).astype(
                jnp.bfloat16
            )

    def gather(b):
        low, high = made[b + 1, :half], made[b + 1, half:]
        cross[0] += dot(low, low, NT)
        cross[1] += dot(high, low, NT)
        cross[2] += dot(high, high, NT)

    read(0).wait()
    multiply(0, 0)

    def several(i, carry):
        b = UNROLL * i
        for k in range(1, UNROLL):
            read(b + k).wait()

        @pl.when(b + UNROLL < blocks)
        def _():
            read(b + UNROLL).wait()

        for k in range(UNROLL):
            following = b + k + 1 if k + 1 < UNROLL else jnp.minimum(b + UNROLL, blocks - 1)
            gather(b + k - 1)
            multiply(following, (k + 1) % 2)
            shape(b + k, k % 2)
        for k in range(UNROLL):
            write(b + k).start()
        return carry

    lax.fori_loop(0, blocks // UNROLL, several, 0)
    gather(blocks - 1)

    keep[...] = jnp.zeros_like(keep)
    send[...] = jnp.zeros_like(send)

    def place(at, values):
        which, row = divmod(at, keep.shape[0])
        for side, out in ((core, keep), (1 - core, send)):

            @pl.when(side == which)
            def _():
                out[row : row + values.shape[0], :] = values

    at = 0
    for b in range(3):
        for c in range(half // LANES):
            place(at, cross[b, :, c * LANES : (c + 1) * LANES])
            at += half
    degrees = []
    for c in range(count // LANES):
        turned = jnp.transpose(column[c * LANES : (c + 1) * LANES, :])
        degrees.append(jnp.sum(turned, axis=0, keepdims=True))
    place(at, jnp.concatenate(degrees, axis=0))

    def finish(b, carry):
        write(b).wait()
        return carry

    lax.fori_loop(0, blocks, finish, 0)


def main_pass(own, other, windows, total_rows, axis):
    rows_here, width = windows.shape
    count = 2 * own.shape[0] * LANES // width
    half = count // 2
    blocks = rows_here // SUB
    return pl.pallas_call(
        functools.partial(main_kernel, axis),
        out_shape=(
            jax.ShapeDtypeStruct((blocks, count, SUB), jnp.bfloat16),
            jax.ShapeDtypeStruct((total_rows // 2, LANES), jnp.float32),
            jax.ShapeDtypeStruct((total_rows // 2, LANES), jnp.float32),
        ),
        in_specs=[
            pl.BlockSpec(memory_space=pltpu.VMEM),
            pl.BlockSpec(memory_space=pltpu.VMEM),
            pl.BlockSpec(memory_space=pl.ANY),
        ],
        out_specs=(
            pl.BlockSpec(memory_space=pl.ANY),
            pl.BlockSpec(memory_space=pltpu.VMEM),
            pl.BlockSpec(memory_space=pltpu.VMEM),
        ),
        scratch_shapes=[
            pltpu.VMEM((count, width), jnp.bfloat16),
            pltpu.VMEM((count, LANES), jnp.float32),
            pltpu.VMEM((blocks, SUB, width), jnp.bfloat16),
            pltpu.VMEM((blocks + 1, count, SUB), jnp.bfloat16),
            pltpu.VMEM((2, count, SUB), jnp.float32),
            pltpu.VMEM((3, half, half), jnp.float32),
            pltpu.VMEM((count, LANES), jnp.float32),
            pltpu.SemaphoreType.DMA((blocks,)),
            pltpu.SemaphoreType.DMA((blocks,)),
        ],
        compiler_params=pltpu.CompilerParams(vmem_limit_bytes=44 * 2**20),
    )(own, other, windows)


def split(values):
    high = values.astype(jnp.bfloat16)
    rest = values - high.astype(jnp.float32)
    middle = rest.astype(jnp.bfloat16)
    low = (rest - middle.astype(jnp.float32)).astype(jnp.bfloat16)
    return high, middle, low


def exact_dot(a, b, dims):
    n = a[0].shape[0]
    high = dot(jnp.concatenate(a, axis=0), b[0], dims)
    middle = dot(jnp.concatenate(a[:2], axis=0), b[1], dims)
    low = dot(a[0], b[2], dims)
    small = high[2 * n :] + middle[n:] + low
    return high[:n] + (high[n : 2 * n] + middle[:n] + small)


def inverse_cholesky(square):
    size = square.shape[0]
    row = lax.broadcasted_iota(jnp.int32, (size, 2 * size), 0)
    lane = lax.broadcasted_iota(jnp.int32, (size, 2 * size), 1)
    table = jnp.concatenate([square, jnp.zeros_like(square)], axis=1)
    diagonal = jnp.sum(jnp.where(lane == row, table, 0.0), axis=1, keepdims=True)
    table = jnp.where(lane == row + size, 1.0, table)
    done, pivots = [], []
    for at in range(0, size, 8):
        left = size - at
        panel = [
            jnp.broadcast_to(table[:, at + j : at + j + 1], (left, 2 * size))
            for j in range(8)
        ]
        for j in range(8):
            pivot = panel[j][j : j + 1]
            pivot_row = table[j : j + 1]
            factor = panel[j] * (1.0 / pivot)
            first = jnp.where(row[:8] > j, factor[:8], 0.0)
            factor = jnp.concatenate([first, factor[8:]], axis=0) if left > 8 else first
            done.append((pivot_row * lax.rsqrt(pivot))[:, size:])
            pivots.append(pivot)
            for q in range(j + 1, 8):
                panel[q] -= factor * panel[q][j : j + 1]
            table -= factor * pivot_row
        table = table[8:]
    return jnp.concatenate(done, axis=0), jnp.concatenate(pivots, axis=0) / diagonal


def embed_kernel(
    axis, own, other, start, scaled, embedding, basis, packed, gram, held, staged, turned, in_sem, out_sem
):
    core = lax.axis_index(axis) % 2
    count = gram.shape[1]
    half = count // 2
    blocks, _, block = held.shape

    def read(b):
        return pltpu.make_async_copy(scaled.at[b], held.at[b], in_sem.at[b])

    def write(b):
        return pltpu.make_async_copy(
            staged.at[:, pl.ds(b * block, block)],
            embedding.at[:, pl.ds(b * block, block)],
            out_sem.at[b],
        )

    for b in range(blocks):
        read(b).start()

    size = own.shape[0]
    packed[pl.ds(pl.multiple_of(core * size, size), size), :] = own[...]
    packed[pl.ds(pl.multiple_of((1 - core) * size, size), size), :] = other[...]
    base = 3 * half * (half // LANES)
    degree = jnp.concatenate(
        [packed[base + c : base + c + 1, :] for c in range(count // LANES)], axis=1
    )
    across = lax.rsqrt(degree)
    down = jnp.concatenate(
        [
            jnp.transpose(
                jnp.broadcast_to(across[:, c * LANES : (c + 1) * LANES], (LANES, LANES))
            )
            for c in range(count // LANES)
        ],
        axis=0,
    )

    def corner(b):
        at = b * half * (half // LANES)
        return jnp.concatenate(
            [packed[at + c * half : at + (c + 1) * half, :] for c in range(half // LANES)],
            axis=1,
        )

    def fill(rows, columns, values):
        for term, part in enumerate(split(values)):
            gram[term, rows, columns] = part

    wide = jnp.concatenate([down] * (half // LANES), axis=1)
    first, second = slice(0, half), slice(half, count)
    side = corner(1) * wide[half:] * across[:, :half]
    fill(first, first, corner(0) * wide[:half] * across[:, :half])
    fill(second, first, side)
    fill(first, second, jnp.transpose(side))
    fill(second, second, corner(2) * wide[half:] * across[:, half:])

    def advance(rows, steps):
        for _ in range(steps):
            rows = exact_dot(split(rows), [gram[0], gram[1], gram[2]], NN)
        terms = split(rows)
        inverse, ratio = inverse_cholesky(exact_dot(terms, terms, NT))
        return exact_dot(split(inverse), terms, NN), ratio

    begin = jnp.transpose(start[...])
    rows, good = begin, None
    for steps, least in GROUPS:
        rows, ratio = advance(rows, steps)
        here = jnp.where(ratio > least, 1.0, 0.0)
        good = here if good is None else good * here
    turned[...] = rows

    @pl.when(jnp.logical_not(jnp.min(good) > 0.5))
    def _():
        turned[...] = lax.fori_loop(0, ITERS, lambda _, rows: advance(rows, 1)[0], begin)

    basis[...] = turned[...]
    weighted = (turned[...] * across).astype(jnp.bfloat16)
    for b in range(blocks):
        read(b).wait()
        staged[:, b * block : (b + 1) * block] = dot(weighted, held[b], NN)
        write(b).start()
    for b in range(blocks):
        write(b).wait()


def embed(own, other, start_basis, scaled, axis):
    blocks, count, block = scaled.shape
    kept = start_basis.shape[1]
    rows_here = blocks * block
    return pl.pallas_call(
        functools.partial(embed_kernel, axis),
        out_shape=(
            jax.ShapeDtypeStruct((kept, rows_here), jnp.float32),
            jax.ShapeDtypeStruct((kept, count), jnp.float32),
        ),
        in_specs=[
            pl.BlockSpec(memory_space=pltpu.VMEM),
            pl.BlockSpec(memory_space=pltpu.VMEM),
            pl.BlockSpec(memory_space=pltpu.VMEM),
            pl.BlockSpec(memory_space=pl.ANY),
        ],
        out_specs=(
            pl.BlockSpec(memory_space=pl.ANY),
            pl.BlockSpec(memory_space=pltpu.VMEM),
        ),
        scratch_shapes=[
            pltpu.VMEM((2 * own.shape[0], LANES), jnp.float32),
            pltpu.VMEM((3, count, count), jnp.bfloat16),
            pltpu.VMEM((blocks, count, block), jnp.bfloat16),
            pltpu.VMEM((kept, rows_here), jnp.float32),
            pltpu.VMEM((kept, count), jnp.float32),
            pltpu.SemaphoreType.DMA((blocks,)),
            pltpu.SemaphoreType.DMA((blocks,)),
        ],
        compiler_params=pltpu.CompilerParams(vmem_limit_bytes=50 * 2**20),
    )(own, other, start_basis, scaled)


def total_over(keep, send, axes, shape):
    rows, sub = shape
    chips = rows // 2 * sub
    cores = [(r, r ^ 1) for r in range(rows)]
    groups = [
        [r * sub + s for r in range(c, rows, 2) for s in range(sub)] for c in range(2)
    ]

    def exchange(values):
        return lax.all_to_all(
            values, axes, 0, 0, axis_index_groups=groups, tiled=True
        )

    values = keep + lax.ppermute(send, axes[0], cores)
    pieces = exchange(values.reshape(chips, keep.shape[0] // chips, LANES))
    mine = jnp.sum(pieces, axis=0)
    own = exchange(jnp.broadcast_to(mine[None], pieces.shape)).reshape(keep.shape)
    return own, lax.ppermute(own, axes[0], cores)


def per_device(shape, windows, landmark_index, start_basis):
    axes = ("rows", "sub")
    own, other = total_over(*pick(landmark_index, windows, axes), axes, shape)
    total_rows = shape[0] * shape[1] * CHUNK
    scaled, keep, send = main_pass(own, other, windows, total_rows, axes[0])
    own, other = total_over(keep, send, axes, shape)
    embedding, turned = embed(own, other, start_basis, scaled, axes[0])
    return embedding, turned.T


def solution(mesh):
    placed = (P(("rows", "sub"), None), P(), P())
    shape = (mesh.shape["rows"], mesh.shape["sub"])
    return jax.shard_map(
        functools.partial(per_device, shape),
        mesh=mesh,
        in_specs=placed,
        out_specs=(P(None, ("rows", "sub")), P()),
        check_vma=False,
    )
```
